256 devices in a mesh: section: 32 (over z_lo, y, x), tp: 8 (over z_hi, core).
Axes of the slice: x: 4, y: 4, z: 8 (z_hi: 4, z_lo: 2; z = z_hi * 2 + z_lo), core: 2. Of those that a mesh axis runs over, the one named last changes fastest.
Arguments:
- hidden_t: bfloat16 [8192, 384], P('tp'), may hold values from -40 to 40
- norm_gain: bfloat16 [8, 8192], replicated, may hold values from 0.099609375 to 1.8984375
- q_weight: bfloat16 [32, 8192, 2048], P('section', None, 'tp'), may hold values from -0.0625 to 0.0625
- k_weight: bfloat16 [32, 2048, 1024], P('section', None, 'tp'), may hold values from -0.0625 to 0.0625
- v_weight: bfloat16 [32, 2048, 1024], P('section', None, 'tp'), may hold values from -0.0625 to 0.0625
- o_weight: bfloat16 [32, 2048, 8192], P('section', 'tp'), may hold values from -0.0625 to 0.0625
- lengths: int32 [32], replicated, may hold values from 1 to 24, 384 in all
- prior_offsets: int32 [32], replicated, may hold values from 0 to 4095
- owners: int32 [32], replicated, may hold values from 0 to 31, each once
Outputs:
- final_hidden: bfloat16 [8192, 384], P('tp', 'section')
- kv_cache: bfloat16 [32, 8, 24, 2048], P('section', None, None, 'tp')
The draws below stay inside these ranges and needn't reach their ends.
Inputs may be any that keep to these rules, and one draw needn't show every extreme that they name: `lengths`: the 32 requests fill all 384 tokens; some request has exactly 24 tokens. `owners`: each owner serves exactly one request.
All inputs are finite; a program needn't handle non-finite values.
Results may differ from the reference program's by a relative error of at most 0.023.
Values may be sent and summed in bfloat16 or wider, within the bound.
No kernel may reach another device: no remote copies, remote signals or barrier semaphores. Data moves between devices by JAX's collectives and lax.ppermute only.
A program may use at most 128 MiB of HBM per device.

```python
import math
import jax
import jax.numpy as jnp
import numpy as np
from jax import lax

D = 8192
HEAD_DIM = 128
QPG = 8
SUBS = 4
TOKENS = 384
MAXPOS = 4096
QSUB = 2
KV_HEADS = 8
LAYERS = 8
REQS = 32
CAP = 24


def draw_hidden_t(key, part):
    key = jax.random.fold_in(key, 7)
    key_base, key_cols = jax.random.split(key, 2)
    col_scale = jnp.exp(jax.random.uniform(key_cols, (1, TOKENS), jnp.float32, 0.0, math.log(10.0)))
    base_vals = jnp.clip(jax.random.normal(key_base, (D, TOKENS), jnp.float32), -4.0, 4.0)
    return (base_vals * col_scale).astype(jnp.bfloat16)


def place_ends(array, own_key, least, largest):
    place = [jax.random.randint(jax.random.fold_in(own_key, axis), (), 0, length) for axis, length in enumerate(array.shape)]
    longest = array.shape.index(max(array.shape))
    neighbour = place[:longest] + [(place[longest] + 1) % array.shape[longest]] + place[longest + 1:]
    return array.at[tuple(place)].set(least).at[tuple(neighbour)].set(largest)


def steps_of(own_key, shape, cuts, least, high):
    gain = 1.0
    for axis_at, blocks in cuts:
        heights = jax.random.uniform(jax.random.fold_in(jax.random.fold_in(own_key, 6), axis_at), (blocks,), jnp.float32, least / len(cuts), high / len(cuts))
        gain = gain * jnp.repeat(jnp.exp(heights), shape[axis_at] // blocks).reshape((-1,) + (1,) * (len(shape) - 1 - axis_at))
    return gain


def profile(number_of, total, reach, slope):
    loads = [(1 << 20) // math.isqrt(rank ** slope) + 1 for rank in range(2, number_of + 1)]
    rest, holding = total - reach - (number_of - 1), [1] * (number_of - 1)
    while rest > 0:
        movable = [i for i in range(number_of - 1) if holding[i] < reach]
        mass, remaining = sum([loads[i] for i in movable]), rest
        for i in movable:
            extra = min(reach - holding[i], max(1, remaining * loads[i] // mass), rest)
            holding[i] = holding[i] + extra
            rest = rest - extra
    return np.array([reach] + holding)


def ragged(stream_key, count, total, reach, slope):
    if count == 2:
        one = jax.random.randint(stream_key, (), max(1, total - reach), min(reach, total - 1) + 1)
        return jnp.stack([one, total - one])
    sizes = jnp.asarray(profile(count, total, reach, slope), jnp.int32)
    twos = (count - 1) // 2
    giver, receiver = sizes[1:1 + 2 * twos:2], sizes[2:2 + 2 * twos:2]
    room = jnp.minimum(giver - 1, reach - receiver)
    shifted = jax.random.randint(jax.random.fold_in(stream_key, 1), (twos,), 0, 1 << 20) % (room + 1)
    sizes = sizes.at[1:1 + 2 * twos:2].set(giver - shifted).at[2:2 + 2 * twos:2].set(receiver + shifted)
    return sizes[jax.random.permutation(jax.random.fold_in(stream_key, 2), count)]


def centred(rng, shape, scale, reach, pieces=(), held_as=jnp.bfloat16):
    loudness = steps_of(rng, shape, pieces, -0.22, 0.18) if pieces else 1.0
    array = jax.random.normal(rng, shape, jnp.float32) * scale * loudness
    return jnp.minimum(jnp.maximum(array, -reach), reach).astype(held_as)


def setup_inputs(seed: int = 0) -> dict:
    arg_keys = jax.random.split(jax.random.key(seed), 10)
    hidden_t = draw_hidden_t(jax.random.fold_in(arg_keys[9], 71), 0)
    norm_gain = jnp.clip(1.0 + 0.18 * jax.random.normal(arg_keys[1], (LAYERS, D), jnp.float32), 0.099609375, 1.8984375).astype(jnp.bfloat16)
    q_weight = centred(arg_keys[2], (LAYERS * SUBS, D, KV_HEADS * QSUB * HEAD_DIM), D ** -0.5, 0.0625, ((0, 32), (2, 8)))
    k_weight = centred(arg_keys[3], (LAYERS * SUBS, D // SUBS, KV_HEADS * HEAD_DIM), D ** -0.5, 0.0625, ((0, 32), (2, 8)))
    v_weight = centred(arg_keys[4], (LAYERS * SUBS, D // SUBS, KV_HEADS * HEAD_DIM), D ** -0.5, 0.0625, ((0, 32), (2, 8)))
    o_weight = centred(arg_keys[5], (LAYERS * SUBS, KV_HEADS * QSUB * HEAD_DIM, D), (KV_HEADS * QPG * HEAD_DIM) ** -0.5, 0.0625, ((0, 32), (1, 8)))
    lengths = ragged(arg_keys[6], REQS, TOKENS, CAP, 2).astype(jnp.int32)
    prior_offsets = place_ends(jax.random.randint(arg_keys[7], (REQS,), 0, MAXPOS), jax.random.fold_in(arg_keys[7], 1), 0, MAXPOS - 1).astype(jnp.int32)
    owners = jax.random.permutation(arg_keys[8], REQS).astype(jnp.int32)
    return dict(hidden_t=hidden_t, norm_gain=norm_gain, q_weight=q_weight, k_weight=k_weight, v_weight=v_weight, o_weight=o_weight, lengths=lengths, prior_offsets=prior_offsets, owners=owners)


NORM_EPS = 1e-05
ROPE_BASE = 500000.0

def rope_tables(positions):
    half_dim = HEAD_DIM // 2
    steps_i = jnp.arange(half_dim, dtype=jnp.float32)
    inv_freq = jnp.power(jnp.float32(ROPE_BASE), -(2.0 * steps_i) / HEAD_DIM)
    angle = positions.astype(jnp.float32)[:, None] * inv_freq[None, :]
    return (jnp.cos(angle)[:, None, :], jnp.sin(angle)[:, None, :])

def rotate_pairs(values, cos_table, sin_table):
    half_dim = values.shape[-1] // 2
    first_half = values[..., :half_dim]
    second_half = values[..., half_dim:]
    return jnp.concatenate([first_half * cos_table - second_half * sin_table, second_half * cos_table + first_half * sin_table], axis=-1)

def reference(hidden_t, norm_gain, q_weight, k_weight, v_weight, o_weight, lengths, prior_offsets, owners):
    tokens = hidden_t.shape[1]
    num_reqs = lengths.shape[0]
    req_ends = jnp.cumsum(lengths).astype(jnp.int32)
    req_starts = (req_ends - lengths).astype(jnp.int32)
    tok_ids = jnp.arange(tokens, dtype=jnp.int32)
    req_of_tok = lax.optimization_barrier(jnp.sum((tok_ids[:, None] >= req_ends[None, :]).astype(jnp.int32), axis=1))
    req_onehot = req_of_tok[:, None] == jnp.arange(num_reqs, dtype=jnp.int32)[None, :]
    positions = lax.optimization_barrier(jnp.sum(jnp.where(req_onehot, (prior_offsets - req_starts)[None, :], 0), axis=1)).astype(jnp.int32) + tok_ids
    key_mask = (req_of_tok[:, None] == req_of_tok[None, :]) & (tok_ids[None, :] <= tok_ids[:, None])
    cos_table, sin_table = rope_tables(positions)
    q_full = q_weight.reshape(LAYERS, SUBS, D, KV_HEADS, QSUB, HEAD_DIM).transpose(0, 2, 3, 1, 4, 5).reshape(LAYERS, D, KV_HEADS * QPG * HEAD_DIM)
    k_full = k_weight.reshape(LAYERS, D, KV_HEADS * HEAD_DIM)
    v_full = v_weight.reshape(LAYERS, D, KV_HEADS * HEAD_DIM)
    o_full = o_weight.reshape(LAYERS, SUBS, KV_HEADS, QSUB, HEAD_DIM, D).transpose(0, 2, 1, 3, 4, 5).reshape(LAYERS, KV_HEADS * QPG * HEAD_DIM, D)

    def layer(h_now, weights):
        gain_row, w_query, w_key, w_value, w_out = weights
        h_float = h_now.astype(jnp.float32)
        mean_square = lax.optimization_barrier(jnp.mean(h_float * h_float, axis=0))
        normed = (h_float * lax.rsqrt(mean_square + NORM_EPS)[None, :] * gain_row.astype(jnp.float32)[:, None]).astype(jnp.bfloat16)
        query_rows = jnp.dot(normed.T, w_query, preferred_element_type=jnp.float32)
        key_rows = jnp.dot(normed.T, w_key, preferred_element_type=jnp.float32)
        value_rows = jnp.dot(normed.T, w_value, preferred_element_type=jnp.float32)
        query_rot = rotate_pairs(query_rows.reshape(tokens, KV_HEADS * QPG, HEAD_DIM), cos_table, sin_table).astype(jnp.bfloat16)
        key_rot = rotate_pairs(key_rows.reshape(tokens, KV_HEADS, HEAD_DIM), cos_table, sin_table).astype(jnp.bfloat16)
        value_new = value_rows.reshape(tokens, KV_HEADS, HEAD_DIM).astype(jnp.bfloat16)
        query_grp = query_rot.reshape(tokens, KV_HEADS, QPG, HEAD_DIM).astype(jnp.float32)
        scores = jnp.einsum('tjgh,sjh->jgts', query_grp, key_rot.astype(jnp.float32)) / math.sqrt(HEAD_DIM)
        exp_scores = jnp.where(key_mask[None, None], jnp.exp(scores), 0.0)
        probs = (exp_scores / lax.optimization_barrier(jnp.sum(exp_scores, axis=-1, keepdims=True))).astype(jnp.bfloat16)
        attended = jnp.einsum('jgts,sjh->tjgh', probs.astype(jnp.float32), value_new.astype(jnp.float32)).astype(jnp.bfloat16)
        attended = attended.reshape(tokens, KV_HEADS, SUBS, QSUB * HEAD_DIM)
        out_groups = w_out.reshape(KV_HEADS, SUBS, QSUB * HEAD_DIM, w_out.shape[1])
        parts = jnp.einsum('tjuq,juqd->judt', attended.astype(jnp.float32), out_groups.astype(jnp.float32)).astype(jnp.bfloat16)
        updated = (h_float + lax.optimization_barrier(jnp.sum(parts.astype(jnp.float32), axis=(0, 1)))).astype(jnp.bfloat16)
        layer_kv = jnp.concatenate([key_rot, value_new], axis=-1).reshape(tokens, KV_HEADS * 2 * HEAD_DIM)
        return (updated, layer_kv)
    final_hidden, all_kv = lax.scan(layer, hidden_t, (norm_gain, q_full, k_full, v_full, o_full))
    owner_onehot = owners[None, :] == jnp.arange(num_reqs, dtype=jnp.int32)[:, None]
    owner_starts = lax.optimization_barrier(jnp.sum(jnp.where(owner_onehot, req_starts[None, :], 0), axis=1))
    owner_lens = lax.optimization_barrier(jnp.sum(jnp.where(owner_onehot, lengths[None, :], 0), axis=1))
    slot_ids = jnp.arange(CAP, dtype=jnp.int32)
    row_index = jnp.minimum(owner_starts[:, None] + slot_ids[None, :], tokens - 1).astype(jnp.int32)
    row_valid = slot_ids[None, :] < owner_lens[:, None]
    picked = all_kv[:, row_index]
    picked = jnp.transpose(picked, (1, 0, 2, 3))
    kv_cache = jnp.where(row_valid[:, None, :, None], picked, jnp.zeros((), jnp.bfloat16))
    return (final_hidden, kv_cache)
```

```python
import math

import jax
import jax.numpy as jnp
from jax import lax
from jax.sharding import Mesh, PartitionSpec as P

HEAD_DIM = 128
NORM_EPS = 1e-05
ROPE_BASE = 500000.0
LAYERS = 8
SUBS = 4
ZH = 4
AXES = ("zl", "y", "x", "zh", "c")
SECTION = ("zl", "y", "x")
TP = ("zh", "c")
PIECES = 4
ROWS = 256
F32 = jnp.float32
BF16 = jnp.bfloat16


def flat(l, x, z, c):
    return ((l * SUBS + x) * ZH + z) * 2 + c


def send(value, layers, target):
    pairs = []
    for l in layers:
        for x in range(SUBS):
            for z in range(ZH):
                for c in range(2):
                    goal = target(l, x, z, c)
                    if goal is not None:
                        pairs.append((flat(l, x, z, c), flat(*goal)))
    return lax.ppermute(value, AXES, pairs)


def over_x(value, layers, d):
    return send(value, layers, lambda l, x, z, c: (l, (x + d) % SUBS, z, c))


def over_z(value, layers, d):
    return send(value, layers, lambda l, x, z, c: (l, x, (z + d) % ZH, c))


def over_core(value, layers):
    return send(value, layers, lambda l, x, z, c: (l, x, z, 1 - c))


def to_next(value, layers):
    return send(value, layers, lambda l, x, z, c: (l + 1, x, z, c) if l + 1 < LAYERS else None)


def rope_tables(positions):
    half_dim = HEAD_DIM // 2
    steps_i = jnp.arange(half_dim, dtype=F32)
    inv_freq = jnp.power(F32(ROPE_BASE), -(2.0 * steps_i) / HEAD_DIM)
    angle = positions.astype(F32)[:, None] * inv_freq[None, :]
    return (jnp.cos(angle), jnp.sin(angle))


def rotate_pairs(values, cos_table, sin_table):
    half_dim = values.shape[-1] // 2
    a = values[..., :half_dim]
    b = values[..., half_dim:]
    return jnp.concatenate([a * cos_table - b * sin_table, b * cos_table + a * sin_table], axis=-1)


def dot(a, b):
    return lax.dot_general(a, b, (((1,), (0,)), ((), ())), preferred_element_type=F32)


def shards(
    hidden_t, norm_gain, q_weight, k_weight, v_weight, o_weight, lengths, prior_offsets, owners
):
    zl = lax.axis_index("zl")
    x = lax.axis_index("x")
    z = lax.axis_index("zh")
    c = lax.axis_index("c")
    layer_idx = zl * 4 + lax.axis_index("y")
    tokens = hidden_t.shape[1]
    features = norm_gain.shape[1]
    quarter = features // SUBS
    span = tokens // PIECES
    num_reqs = lengths.shape[0]
    every = range(LAYERS)

    req_ends = jnp.cumsum(lengths)
    req_starts = req_ends - lengths
    tok_ids = jnp.arange(tokens, dtype=jnp.int32)
    req_ids = jnp.arange(num_reqs, dtype=jnp.int32)
    req_of_tok = jnp.sum((tok_ids[:, None] >= req_ends[None, :]).astype(jnp.int32), axis=1)
    req_onehot = req_of_tok[:, None] == req_ids[None, :]
    positions = (
        jnp.sum(jnp.where(req_onehot, (prior_offsets - req_starts)[None, :], 0), axis=1) + tok_ids
    )
    key_mask = (req_of_tok[:, None] == req_of_tok[None, :]) & (tok_ids[None, :] <= tok_ids[:, None])
    cos_table, sin_table = rope_tables(positions)

    hid = hidden_t.T
    share0 = None
    for k in range(4):
        got = send(
            hid[:, k * ROWS : (k + 1) * ROWS],
            [0],
            lambda l, xx, zz, cc: (l, xx, 2 * cc + k // 2, k % 2) if zz == xx else None,
        )
        share0 = got if share0 is None else share0 + got

    w_query = q_weight[0]
    w_out = o_weight[0]
    q_blocks = [None] * SUBS
    o_blocks = [None] * SUBS
    for d in range(SUBS):
        start = ((x + d) % SUBS) * quarter
        block = lax.dynamic_slice_in_dim(w_query, start, quarter, 0)
        q_blocks[(-d) % SUBS] = over_x(block, every, d) if d else block
    for d in range(SUBS):
        start = ((x + d) % SUBS) * quarter
        block = lax.dynamic_slice_in_dim(w_out, start, quarter, 1)
        o_blocks[(-d) % SUBS] = over_x(block, every, d) if d else block
    in_order = [((z - dz) % ZH) * 2 + (c ^ dc) for dc in range(2) for dz in range(ZH)]
    w_in = jnp.concatenate(q_blocks + [k_weight[0], v_weight[0]], axis=1)
    w_in = jnp.concatenate(
        [lax.dynamic_slice_in_dim(w_in, t * ROWS, ROWS, 0) for t in in_order], axis=0
    )
    out_order = [((z + dz) % ZH) * 2 + (c ^ dc) for dc in range(2) for dz in range(ZH)]
    w_back = jnp.concatenate(o_blocks, axis=0)
    w_back = jnp.concatenate(
        [lax.dynamic_slice_in_dim(w_back, t * ROWS, ROWS, 1) for t in out_order], axis=1
    )
    gain_row = lax.dynamic_index_in_dim(norm_gain, layer_idx, 0, keepdims=False)
    gain = jnp.concatenate(
        [lax.dynamic_slice_in_dim(gain_row, x * quarter + t * ROWS, ROWS, 0) for t in in_order]
    ).astype(F32)

    kv_buf = jnp.zeros((tokens, 2 * HEAD_DIM), BF16)
    received = jnp.zeros((span, ROWS), BF16)
    last_parts = []
    for step in range(LAYERS + PIECES - 1):
        layers = every
        micro_raw = step - layer_idx
        active = (micro_raw >= 0) & (micro_raw < PIECES)
        col_start = jnp.clip(micro_raw, 0, PIECES - 1) * span
        share = received
        if step < PIECES:
            share = jnp.where(layer_idx == 0, share0[step * span : (step + 1) * span], received)

        own_core = [share] + [over_z(share, layers, d) for d in range(1, ZH)]
        own_core = jnp.concatenate(own_core, axis=1)
        whole = jnp.concatenate([own_core, over_core(own_core, layers)], axis=1)

        h_float = whole.astype(F32)
        squares = jnp.sum(h_float * h_float, axis=1)
        scaled = (h_float * gain[None, :]).astype(BF16)
        parts = dot(scaled, w_in)
        sent = parts.astype(BF16)
        high = squares.astype(BF16)
        low = (squares - high.astype(F32)).astype(BF16)
        extra = jnp.pad(jnp.stack([high, low]), ((0, 14), (0, 4 * HEAD_DIM - span)))
        qkv = jnp.concatenate([parts[:, :ROWS], parts[:, SUBS * ROWS :]], axis=1)
        for d in range(1, SUBS):
            payload = jnp.concatenate(
                [sent[:, d * ROWS : (d + 1) * ROWS], sent[:, SUBS * ROWS :]], axis=1
            )
            got = over_x(jnp.concatenate([payload, extra], axis=0), layers, d).astype(F32)
            qkv = qkv + got[:span]
            squares = squares + got[span, :span] + got[span + 1, :span]
        qkv = qkv * lax.rsqrt(squares / features + NORM_EPS)[:, None]

        cos_now = lax.dynamic_slice_in_dim(cos_table, col_start, span, 0)
        sin_now = lax.dynamic_slice_in_dim(sin_table, col_start, span, 0)
        mask_now = lax.dynamic_slice_in_dim(key_mask, col_start, span, 0)
        query = [
            rotate_pairs(qkv[:, i * HEAD_DIM : (i + 1) * HEAD_DIM], cos_now, sin_now).astype(BF16)
            for i in range(2)
        ]
        key_new = rotate_pairs(qkv[:, 2 * HEAD_DIM : 3 * HEAD_DIM], cos_now, sin_now).astype(BF16)
        kv_new = jnp.concatenate([key_new, qkv[:, 3 * HEAD_DIM :].astype(BF16)], axis=1)
        kv_now = lax.dynamic_update_slice_in_dim(kv_buf, kv_new, col_start, 0)
        kv_buf = jnp.where(active, kv_now, kv_buf)
        heads = []
        for i in range(2):
            scores = lax.dot_general(
                query[i],
                kv_now[:, :HEAD_DIM],
                (((1,), (1,)), ((), ())),
                preferred_element_type=F32,
            ) / math.sqrt(HEAD_DIM)
            exp_scores = jnp.where(mask_now, jnp.exp(scores), 0.0)
            probs = (exp_scores / jnp.sum(exp_scores, axis=-1, keepdims=True)).astype(BF16)
            heads.append(dot(probs, kv_now[:, HEAD_DIM:]).astype(BF16))
        attended = jnp.concatenate(heads, axis=1)

        heads = [None] * SUBS
        for d in range(SUBS):
            heads[(-d) % SUBS] = over_x(attended, layers, d) if d else attended
        terms = dot(jnp.concatenate(heads, axis=1), w_back)
        half = ZH * ROWS
        summed = terms[:, :half] + over_core(terms[:, half:].astype(BF16), layers).astype(F32)
        total = share.astype(F32) + summed[:, :ROWS]
        for d in range(1, ZH):
            part = summed[:, d * ROWS : (d + 1) * ROWS].astype(BF16)
            total = total + over_z(part, layers, d).astype(F32)
        updated = total.astype(BF16)
        if step >= LAYERS - 1:
            last_parts.append(updated)
        received = to_next(updated, layers)

    slots = 2 * tokens // num_reqs
    own_slots = slots // SUBS
    owner_onehot = owners[None, :] == req_ids[:, None]
    owner_starts = jnp.sum(jnp.where(owner_onehot, req_starts[None, :], 0), axis=1)
    owner_lens = jnp.sum(jnp.where(owner_onehot, lengths[None, :], 0), axis=1)
    slot_ids = x * own_slots + jnp.arange(own_slots, dtype=jnp.int32)
    row_index = jnp.where(
        slot_ids[None, :] < owner_lens[:, None], owner_starts[:, None] + slot_ids[None, :], tokens
    ).reshape(-1)
    pick = (row_index[:, None] == tok_ids[None, :]).astype(BF16)
    kv_out = dot(pick, kv_buf).astype(BF16).reshape(num_reqs, own_slots, 2 * HEAD_DIM)
    h_last = jnp.concatenate(last_parts, axis=0).reshape(num_reqs, tokens // num_reqs, ROWS)
    mixed = lax.all_to_all(jnp.concatenate([kv_out, h_last], axis=1), SECTION, 0, 0)
    kv_cache = mixed[:, :own_slots].reshape(1, LAYERS, slots, 2 * HEAD_DIM)
    h_four = mixed[(LAYERS - 1) * SUBS :, own_slots:]
    by_tp = lax.all_to_all(jnp.repeat(h_four, 2, axis=0), TP, 0, 0)
    mine = lax.dynamic_slice_in_dim(by_tp, 4 * c, 4, 0)
    final_hidden = mine.transpose(0, 2, 1).reshape(4 * ROWS, tokens // num_reqs)
    return (final_hidden, kv_cache)


def solution(mesh):
    split = Mesh(mesh.devices.reshape(2, 4, SUBS, ZH, 2), AXES)
    return jax.shard_map(
        shards,
        mesh=split,
        in_specs=(
            P(TP, None),
            P(),
            P(SECTION, None, TP),
            P(SECTION, None, TP),
            P(SECTION, None, TP),
            P(SECTION, TP, None),
            P(),
            P(),
            P(),
        ),
        out_specs=(P(TP, SECTION), P(SECTION, None, None, TP)),
        check_vma=False,
    )
```

```python
import math

import jax
import jax.numpy as jnp
from jax import lax
from jax.experimental import pallas as pl
from jax.experimental.pallas import tpu as pltpu
from jax.sharding import Mesh, PartitionSpec as P

HEAD_DIM = 128
NORM_EPS = 1e-05
ROPE_BASE = 500000.0
LAYERS = 8
SUBS = 4
ZH = 4
AXES = ("zl", "y", "x", "zh", "c")
SECTION = ("zl", "y", "x")
TP = ("zh", "c")
PIECES = 3
ROWS = 256
F32 = jnp.float32
BF16 = jnp.bfloat16


def flat(l, x, z, c):
    return ((l * SUBS + x) * ZH + z) * 2 + c


def send(value, layers, target):
    pairs = []
    for l in layers:
        for x in range(SUBS):
            for z in range(ZH):
                for c in range(2):
                    goal = target(l, x, z, c)
                    if goal is not None:
                        pairs.append((flat(l, x, z, c), flat(*goal)))
    return lax.ppermute(value, AXES, pairs)


def over_x(value, layers, d):
    return send(value, layers, lambda l, x, z, c: (l, (x + d) % SUBS, z, c))


def over_z(value, layers, d):
    return send(value, layers, lambda l, x, z, c: (l, x, (z + d) % ZH, c))


def over_core(value, layers):
    return send(value, layers, lambda l, x, z, c: (l, x, z, 1 - c))


def to_next(value, d):
    return send(
        value, range(LAYERS), lambda l, x, z, c: ((l + 1) % LAYERS, x, (z + d) % ZH, c)
    )


def rope_tables(positions):
    half_dim = HEAD_DIM // 2
    steps_i = jnp.arange(half_dim, dtype=F32)
    inv_freq = jnp.power(F32(ROPE_BASE), -(2.0 * steps_i) / HEAD_DIM)
    angle = positions.astype(F32)[:, None] * inv_freq[None, :]
    return (jnp.cos(angle), jnp.sin(angle))


def rotate_pairs(values, cos_table, sin_table):
    half_dim = values.shape[-1] // 2
    a = values[..., :half_dim]
    b = values[..., half_dim:]
    return jnp.concatenate([a * cos_table - b * sin_table, b * cos_table + a * sin_table], axis=-1)


def dot(a, b):
    return lax.dot_general(a, b, (((1,), (0,)), ((), ())), preferred_element_type=F32)


def rearrange_kernel(axis, count, starts, source, *rest):
    outs, sems = rest[:count], rest[count]
    copies = []
    per = outs[0].shape[axis] // ROWS
    for i in range(count * per):
        at = pl.ds(pl.multiple_of(starts[i], ROWS), ROWS)
        to = pl.ds((i % per) * ROWS, ROWS)
        src = source.at[at] if axis == 0 else source.at[:, at]
        out = outs[i // per]
        dst = out.at[to] if axis == 0 else out.at[:, to]
        copies.append(pltpu.make_async_copy(src, dst, sems.at[i]))
    for copy in copies:
        copy.start()
    for copy in copies:
        copy.wait()


def rearrange(source, starts, axis, shape, count):
    total = len(starts)
    return pl.pallas_call(
        lambda *refs: rearrange_kernel(axis, count, *refs),
        out_shape=[jax.ShapeDtypeStruct(shape, source.dtype)] * count,
        in_specs=[pl.BlockSpec(memory_space=pltpu.SMEM), pl.BlockSpec(memory_space=pl.ANY)],
        out_specs=[pl.BlockSpec(memory_space=pl.ANY)] * count,
        scratch_shapes=[pltpu.SemaphoreType.DMA((total,))],
        cost_estimate=pl.CostEstimate(
            flops=0, bytes_accessed=2 * source.size * source.dtype.itemsize, transcendentals=0
        ),
    )(jnp.stack(starts).astype(jnp.int32), source)


def project_kernel(own, other, gain, q0, q1, q2, q3, kv, mine, pay1, pay2, pay3, sums):
    span, half = own.shape
    halves = [own[...].astype(F32), other[...].astype(F32)]
    squares = sum(jnp.sum(h * h, axis=1, keepdims=True) for h in halves)
    scaled = [
        (h * gain[:, i * half : (i + 1) * half]).astype(BF16) for i, h in enumerate(halves)
    ]

    def product(weights):
        return sum(
            jnp.dot(a, weights[i * half : (i + 1) * half, :], preferred_element_type=F32)
            for i, a in enumerate(scaled)
        )

    kv_part = product(kv)
    kv_sent = kv_part.astype(BF16)
    mine[:, :ROWS] = product(q0)
    mine[:, ROWS:] = kv_part
    across = jnp.transpose(jnp.broadcast_to(squares, (span, 128)))[:16]
    sums[...] = across[:8]
    high = across.astype(BF16)
    low = (across - high.astype(F32)).astype(BF16)
    row = lax.broadcasted_iota(jnp.int32, (16, span), 0)
    extra = jnp.where(row == 0, high.astype(F32), jnp.where(row == 1, low.astype(F32), 0.0))
    for pay, weights in ((pay1, q1), (pay2, q2), (pay3, q3)):
        pay[:span, :ROWS] = product(weights).astype(BF16)
        pay[:span, ROWS:] = kv_sent
        pay[span:, :] = jnp.zeros((16, 2 * ROWS), BF16)
        pay[span:, :span] = extra.astype(BF16)


def project(own, other, gain, q_blocks, w_kv):
    span = own.shape[0]
    features = w_kv.shape[0]
    payload = jax.ShapeDtypeStruct((span + 16, 2 * ROWS), BF16)
    return pl.pallas_call(
        project_kernel,
        out_shape=[
            jax.ShapeDtypeStruct((span, 2 * ROWS), F32),
            payload,
            payload,
            payload,
            jax.ShapeDtypeStruct((8, span), F32),
        ],
        in_specs=[pl.BlockSpec(memory_space=pltpu.VMEM)] * 8,
        out_specs=[pl.BlockSpec(memory_space=pltpu.VMEM)] * 5,
        compiler_params=pltpu.CompilerParams(vmem_limit_bytes=24 * 2**20),
        cost_estimate=pl.CostEstimate(
            flops=2 * span * features * 5 * ROWS,
            bytes_accessed=2 * features * 5 * ROWS,
            transcendentals=0,
        ),
    )(own, other, gain, *q_blocks, w_kv)


def shards(
    hidden_t, norm_gain, q_weight, k_weight, v_weight, o_weight, lengths, prior_offsets, owners
):
    zl = lax.axis_index("zl")
    x = lax.axis_index("x")
    z = lax.axis_index("zh")
    c = lax.axis_index("c")
    layer_idx = zl * 4 + lax.axis_index("y")
    tokens = hidden_t.shape[1]
    features = norm_gain.shape[1]
    quarter = features // SUBS
    span = tokens // PIECES
    num_reqs = lengths.shape[0]
    every = range(LAYERS)

    req_ends = jnp.cumsum(lengths)
    req_starts = req_ends - lengths
    tok_ids = jnp.arange(tokens, dtype=jnp.int32)
    req_ids = jnp.arange(num_reqs, dtype=jnp.int32)
    req_of_tok = jnp.sum((tok_ids[:, None] >= req_ends[None, :]).astype(jnp.int32), axis=1)
    req_onehot = req_of_tok[:, None] == req_ids[None, :]
    positions = (
        jnp.sum(jnp.where(req_onehot, (prior_offsets - req_starts)[None, :], 0), axis=1) + tok_ids
    )
    key_mask = (req_of_tok[:, None] == req_of_tok[None, :]) & (tok_ids[None, :] <= tok_ids[:, None])
    cos_table, sin_table = rope_tables(positions)

    w_query = q_weight[0]
    out_order = [((z + dz) % ZH) * 2 + (c ^ dc) for dc in range(2) for dz in range(ZH)]
    starts = [((x + d) % SUBS) * quarter + t * ROWS for d in range(SUBS) for t in out_order]
    o_send = rearrange(o_weight[0], starts, 1, (ROWS, quarter), SUBS)
    hidden_t, o_send = lax.optimization_barrier((hidden_t, o_send))
    o_blocks = [None] * SUBS
    for d in range(SUBS):
        o_blocks[(-d) % SUBS] = over_x(o_send[d], every, d) if d else o_send[d]
    hid = hidden_t.T
    first = hid[:span]
    near = [first] + [over_z(first, [0], d) for d in range(1, ZH)]
    far = [over_core(piece, [0]) for piece in near]
    in_order = [((z - dz) % ZH) * 2 + (c ^ dc) for dc in range(2) for dz in range(ZH)]
    starts = [((x + d) % SUBS) * quarter + t * ROWS for d in range(SUBS) for t in in_order]
    q_send = rearrange(w_query, starts, 0, (quarter, ROWS), SUBS)
    q_send, o_blocks = lax.optimization_barrier((q_send, o_blocks))
    q_blocks = [None] * SUBS
    for d in range(SUBS):
        q_blocks[(-d) % SUBS] = over_x(q_send[d], every, d) if d else q_send[d]
    w_back = jnp.concatenate(o_blocks, axis=0)
    w_kv = jnp.concatenate([k_weight[0], v_weight[0]], axis=1)
    w_kv_later = jnp.concatenate(
        [lax.dynamic_slice_in_dim(w_kv, t * ROWS, ROWS, 0) for t in in_order], axis=0
    )
    gain_row = lax.dynamic_index_in_dim(norm_gain, layer_idx, 0, keepdims=False)
    gain = jnp.concatenate(
        [lax.dynamic_slice_in_dim(gain_row, x * quarter + t * ROWS, ROWS, 0) for t in in_order]
    ).astype(F32)[None, :]
    fed = None
    if PIECES > 1:
        for k in range(4):
            got = send(
                hid[span:, k * ROWS : (k + 1) * ROWS],
                [LAYERS - 1],
                lambda l, xx, zz, cc: (l, xx, 2 * cc + k // 2, k % 2) if zz == xx else None,
            )
            fed = got if fed is None else fed + got

    def first_projections():
        squares = jnp.zeros((span,), F32)
        query = jnp.zeros((span, ROWS), F32)
        block = 4 * ROWS
        for piece, t in zip(near + far, in_order):
            now = piece.astype(F32)
            squares = squares + jnp.sum(now * now, axis=1)
            gain_now = lax.dynamic_slice_in_dim(gain_row, t * block, block, 0).astype(F32)
            scaled = (now * gain_now[None, :]).astype(BF16)
            query = query + dot(scaled, lax.dynamic_slice_in_dim(w_query, t * block, block, 0))
        place = (z - x) % ZH
        own = []
        for pieces in (near, far):
            own.append(lax.select_n(place, *pieces))
        own = jnp.concatenate(
            [jnp.where(c == 0, own[0], own[1]), jnp.where(c == 0, own[1], own[0])], axis=1
        )
        gain_own = lax.dynamic_slice_in_dim(gain_row, x * quarter, quarter, 0).astype(F32)
        scaled = (own.astype(F32) * gain_own[None, :]).astype(BF16)
        kv = dot(scaled, w_kv)
        sent, _ = lax.optimization_barrier((kv.astype(BF16), o_blocks))
        for d in range(1, SUBS):
            kv = kv + over_x(sent, every, d).astype(F32)
        share = lax.dynamic_slice_in_dim(own, (z * 2 + c) * ROWS, ROWS, 1)
        return share, jnp.concatenate([query, kv], axis=1), squares

    def projections(pieces):
        own_core = jnp.concatenate(pieces, axis=1)
        other = over_core(own_core, every)
        qkv, *payloads, sums = project(own_core, other, gain, q_blocks, w_kv_later)
        squares = sums[0]
        for d in range(1, SUBS):
            got = over_x(payloads[d - 1], every, d).astype(F32)
            qkv = qkv + got[:span]
            squares = squares + got[span, :span] + got[span + 1, :span]
        return pieces[0], qkv, squares

    kv_buf = jnp.zeros((tokens, 2 * HEAD_DIM), BF16)
    pieces = None
    last_parts = []
    for step in range(LAYERS + PIECES - 1):
        micro_raw = step - layer_idx
        active = (micro_raw >= 0) & (micro_raw < PIECES)
        col_start = jnp.clip(micro_raw, 0, PIECES - 1) * span
        share, qkv, squares = projections(pieces) if step else first_projections()
        qkv = qkv * lax.rsqrt(squares / features + NORM_EPS)[:, None]

        cos_now = lax.dynamic_slice_in_dim(cos_table, col_start, span, 0)
        sin_now = lax.dynamic_slice_in_dim(sin_table, col_start, span, 0)
        mask_now = lax.dynamic_slice_in_dim(key_mask, col_start, span, 0)
        query = [
            rotate_pairs(qkv[:, i * HEAD_DIM : (i + 1) * HEAD_DIM], cos_now, sin_now).astype(BF16)
            for i in range(2)
        ]
        key_new = rotate_pairs(qkv[:, 2 * HEAD_DIM : 3 * HEAD_DIM], cos_now, sin_now).astype(BF16)
        kv_new = jnp.concatenate([key_new, qkv[:, 3 * HEAD_DIM :].astype(BF16)], axis=1)
        kv_now = lax.dynamic_update_slice_in_dim(kv_buf, kv_new, col_start, 0)
        kv_buf = jnp.where(active, kv_now, kv_buf)
        heads = []
        for i in range(2):
            scores = lax.dot_general(
                query[i],
                kv_now[:, :HEAD_DIM],
                (((1,), (1,)), ((), ())),
                preferred_element_type=F32,
            ) / math.sqrt(HEAD_DIM)
            exp_scores = jnp.where(mask_now, jnp.exp(scores), 0.0)
            probs = (exp_scores / jnp.sum(exp_scores, axis=-1, keepdims=True)).astype(BF16)
            heads.append(dot(probs, kv_now[:, HEAD_DIM:]).astype(BF16))
        attended = jnp.concatenate(heads, axis=1)

        heads = [None] * SUBS
        for d in range(SUBS):
            heads[(-d) % SUBS] = over_x(attended, every, d) if d else attended
        terms = dot(jnp.concatenate(heads, axis=1), w_back)
        half = ZH * ROWS
        summed = terms[:, :half] + over_core(terms[:, half:].astype(BF16), every).astype(F32)
        total = share.astype(F32) + summed[:, :ROWS]
        for d in range(1, ZH):
            part = summed[:, d * ROWS : (d + 1) * ROWS].astype(BF16)
            total = total + over_z(part, every, d).astype(F32)
        updated = total.astype(BF16)
        if step >= LAYERS - 1:
            last_parts.append(updated)
        if step < PIECES - 1:
            updated = jnp.where(
                layer_idx == LAYERS - 1, fed[step * span : (step + 1) * span], updated
            )
        if step < LAYERS + PIECES - 2:
            pieces = [to_next(updated, d) for d in range(ZH)]

    slots = 2 * tokens // num_reqs
    own_slots = slots // SUBS
    owner_onehot = owners[None, :] == req_ids[:, None]
    owner_starts = jnp.sum(jnp.where(owner_onehot, req_starts[None, :], 0), axis=1)
    owner_lens = jnp.sum(jnp.where(owner_onehot, lengths[None, :], 0), axis=1)
    slot_ids = x * own_slots + jnp.arange(own_slots, dtype=jnp.int32)
    row_index = jnp.where(
        slot_ids[None, :] < owner_lens[:, None], owner_starts[:, None] + slot_ids[None, :], tokens
    ).reshape(-1)
    pick = (row_index[:, None] == tok_ids[None, :]).astype(BF16)
    kv_out = dot(pick, kv_buf).astype(BF16).reshape(num_reqs, own_slots, 2 * HEAD_DIM)
    h_last = jnp.concatenate(last_parts, axis=0).reshape(num_reqs, tokens // num_reqs, ROWS)
    mixed = lax.all_to_all(jnp.concatenate([kv_out, h_last], axis=1), SECTION, 0, 0)
    kv_cache = mixed[:, :own_slots].reshape(1, LAYERS, slots, 2 * HEAD_DIM)
    h_four = mixed[(LAYERS - 1) * SUBS :, own_slots:]
    by_tp = lax.all_to_all(jnp.repeat(h_four, 2, axis=0), TP, 0, 0)
    mine = lax.dynamic_slice_in_dim(by_tp, 4 * c, 4, 0)
    final_hidden = mine.transpose(0, 2, 1).reshape(4 * ROWS, tokens // num_reqs)
    return (final_hidden, kv_cache)


def solution(mesh):
    split = Mesh(mesh.devices.reshape(2, 4, SUBS, ZH, 2), AXES)
    return jax.shard_map(
        shards,
        mesh=split,
        in_specs=(
            P(TP, None),
            P(),
            P(SECTION, None, TP),
            P(SECTION, None, TP),
            P(SECTION, None, TP),
            P(SECTION, TP, None),
            P(),
            P(),
            P(),
        ),
        out_specs=(P(TP, SECTION), P(SECTION, None, None, TP)),
        check_vma=False,
    )
```

```python
import math

import jax
import jax.numpy as jnp
from jax import lax
from jax.experimental import pallas as pl
from jax.experimental.pallas import tpu as pltpu
from jax.sharding import Mesh, PartitionSpec as P

HEAD_DIM = 128
NORM_EPS = 1e-05
ROPE_BASE = 500000.0
LAYERS = 8
SUBS = 4
ZH = 4
AXES = ("zl", "y", "x", "zh", "c")
SECTION = ("zl", "y", "x")
TP = ("zh", "c")
PIECES = 3
ROWS = 256
F32 = jnp.float32
BF16 = jnp.bfloat16


def flat(l, x, z, c):
    return ((l * SUBS + x) * ZH + z) * 2 + c


def send(value, layers, target):
    pairs = []
    for l in layers:
        for x in range(SUBS):
            for z in range(ZH):
                for c in range(2):
                    goal = target(l, x, z, c)
                    if goal is not None:
                        pairs.append((flat(l, x, z, c), flat(*goal)))
    return lax.ppermute(value, AXES, pairs)


def over_x(value, layers, d):
    return send(value, layers, lambda l, x, z, c: (l, (x + d) % SUBS, z, c))


def over_z(value, layers, d):
    return send(value, layers, lambda l, x, z, c: (l, x, (z + d) % ZH, c))


def over_core(value, layers):
    return send(value, layers, lambda l, x, z, c: (l, x, z, 1 - c))


def to_next(value, d):
    return send(
        value, range(LAYERS), lambda l, x, z, c: ((l + 1) % LAYERS, x, (z + d) % ZH, c)
    )


def rope_tables(positions):
    half_dim = HEAD_DIM // 2
    steps_i = jnp.arange(half_dim, dtype=F32)
    inv_freq = jnp.power(F32(ROPE_BASE), -(2.0 * steps_i) / HEAD_DIM)
    angle = positions.astype(F32)[:, None] * inv_freq[None, :]
    return (jnp.cos(angle), jnp.sin(angle))


def rotate_pairs(values, cos_table, sin_table):
    half_dim = values.shape[-1] // 2
    a = values[..., :half_dim]
    b = values[..., half_dim:]
    return jnp.concatenate([a * cos_table - b * sin_table, b * cos_table + a * sin_table], axis=-1)


def dot(a, b):
    return lax.dot_general(a, b, (((1,), (0,)), ((), ())), preferred_element_type=F32)


def rearrange_kernel(axis, count, starts, source, *rest):
    outs, held, sems, out_sems = rest[:count], rest[count], rest[count + 1], rest[count + 2]
    per = outs[0].shape[axis] // ROWS
    arriving = []
    for i in range(count * per):
        at = pl.ds(pl.multiple_of(starts[i], ROWS), ROWS)
        to = pl.ds((i % per) * ROWS, ROWS)
        src = source.at[at] if axis == 0 else source.at[:, at]
        dst = held.at[i // per, to] if axis == 0 else held.at[i // per, :, to]
        arriving.append(pltpu.make_async_copy(src, dst, sems.at[i]))
        arriving[i].start()
    leaving = []
    for d in range(count):
        for i in range(d * per, (d + 1) * per):
            arriving[i].wait()
        leaving.append(pltpu.make_async_copy(held.at[d], outs[d], out_sems.at[d]))
        leaving[d].start()
    for copy in leaving:
        copy.wait()


def rearrange(source, starts, axis, shape, count):
    total = len(starts)
    return pl.pallas_call(
        lambda *refs: rearrange_kernel(axis, count, *refs),
        out_shape=[jax.ShapeDtypeStruct(shape, source.dtype)] * count,
        in_specs=[pl.BlockSpec(memory_space=pltpu.SMEM), pl.BlockSpec(memory_space=pl.ANY)],
        out_specs=[pl.BlockSpec(memory_space=pl.ANY)] * count,
        scratch_shapes=[
            pltpu.VMEM((count,) + shape, source.dtype),
            pltpu.SemaphoreType.DMA((total,)),
            pltpu.SemaphoreType.DMA((count,)),
        ],
        compiler_params=pltpu.CompilerParams(vmem_limit_bytes=8 * 2**20),
        cost_estimate=pl.CostEstimate(
            flops=0, bytes_accessed=2 * source.size * source.dtype.itemsize, transcendentals=0
        ),
    )(jnp.stack(starts).astype(jnp.int32), source)


def project_kernel(
    own, other, gain, q0, q1, q2, q3, kv, mine, pay1, pay2, pay3, sums, held, sems
):
    span, half = own.shape
    copies = [
        pltpu.make_async_copy(weights, held.at[i], sems.at[i])
        for i, weights in enumerate((kv, q1, q2, q3, q0))
    ]
    for copy in copies:
        copy.start()
    halves = [own[...].astype(F32), other[...].astype(F32)]
    squares = sum(jnp.sum(h * h, axis=1, keepdims=True) for h in halves)
    scaled = [
        (h * gain[:, i * half : (i + 1) * half]).astype(BF16) for i, h in enumerate(halves)
    ]

    def product(at):
        copies[at].wait()
        return sum(
            jnp.dot(a, held[at, i * half : (i + 1) * half, :], preferred_element_type=F32)
            for i, a in enumerate(scaled)
        )

    kv_part = product(0)
    kv_sent = kv_part.astype(BF16)
    mine[:, ROWS:] = kv_part
    across = jnp.transpose(jnp.broadcast_to(squares, (span, 128)))[:16]
    sums[...] = across[:8]
    high = across.astype(BF16)
    low = (across - high.astype(F32)).astype(BF16)
    row = lax.broadcasted_iota(jnp.int32, (16, span), 0)
    extra = jnp.where(row == 0, high.astype(F32), jnp.where(row == 1, low.astype(F32), 0.0))
    for i, pay in enumerate((pay1, pay2, pay3)):
        pay[:span, :ROWS] = product(i + 1).astype(BF16)
        pay[:span, ROWS:] = kv_sent
        pay[span:, :] = jnp.zeros((16, 2 * ROWS), BF16)
        pay[span:, :span] = extra.astype(BF16)
    mine[:, :ROWS] = product(4)


def project(own, other, gain, q_blocks, w_kv):
    span = own.shape[0]
    features = w_kv.shape[0]
    payload = jax.ShapeDtypeStruct((span + 16, 2 * ROWS), BF16)
    return pl.pallas_call(
        project_kernel,
        out_shape=[
            jax.ShapeDtypeStruct((span, 2 * ROWS), F32),
            payload,
            payload,
            payload,
            jax.ShapeDtypeStruct((8, span), F32),
        ],
        in_specs=[pl.BlockSpec(memory_space=pltpu.VMEM)] * 3
        + [pl.BlockSpec(memory_space=pl.ANY)] * 5,
        out_specs=[pl.BlockSpec(memory_space=pltpu.VMEM)] * 5,
        scratch_shapes=[
            pltpu.VMEM((5, features, ROWS), BF16),
            pltpu.SemaphoreType.DMA((5,)),
        ],
        compiler_params=pltpu.CompilerParams(vmem_limit_bytes=24 * 2**20),
        cost_estimate=pl.CostEstimate(
            flops=2 * span * features * 5 * ROWS,
            bytes_accessed=2 * features * 5 * ROWS,
            transcendentals=0,
        ),
    )(own, other, gain, *q_blocks, w_kv)


def shards(
    hidden_t, norm_gain, q_weight, k_weight, v_weight, o_weight, lengths, prior_offsets, owners
):
    zl = lax.axis_index("zl")
    x = lax.axis_index("x")
    z = lax.axis_index("zh")
    c = lax.axis_index("c")
    layer_idx = zl * 4 + lax.axis_index("y")
    tokens = hidden_t.shape[1]
    features = norm_gain.shape[1]
    quarter = features // SUBS
    span = tokens // PIECES
    num_reqs = lengths.shape[0]
    every = range(LAYERS)

    req_ends = jnp.cumsum(lengths)
    req_starts = req_ends - lengths
    tok_ids = jnp.arange(tokens, dtype=jnp.int32)
    req_ids = jnp.arange(num_reqs, dtype=jnp.int32)
    req_of_tok = jnp.sum((tok_ids[:, None] >= req_ends[None, :]).astype(jnp.int32), axis=1)
    req_onehot = req_of_tok[:, None] == req_ids[None, :]
    positions = (
        jnp.sum(jnp.where(req_onehot, (prior_offsets - req_starts)[None, :], 0), axis=1) + tok_ids
    )
    key_mask = (req_of_tok[:, None] == req_of_tok[None, :]) & (tok_ids[None, :] <= tok_ids[:, None])
    cos_table, sin_table = rope_tables(positions)

    w_query = q_weight[0]
    out_order = [((z + dz) % ZH) * 2 + (c ^ dc) for dc in range(2) for dz in range(ZH)]
    starts = [((x + d) % SUBS) * quarter + t * ROWS for d in range(SUBS) for t in out_order]
    o_send = rearrange(o_weight[0], starts, 1, (ROWS, quarter), SUBS)
    hidden_t, o_send = lax.optimization_barrier((hidden_t, o_send))
    o_blocks = [None] * SUBS
    for d in range(SUBS):
        o_blocks[(-d) % SUBS] = over_x(o_send[d], every, d) if d else o_send[d]
    hid = hidden_t.T
    first = hid[:span]
    near = [first] + [over_z(first, [0], d) for d in range(1, ZH)]
    far = [over_core(piece, [0]) for piece in near]
    in_order = [((z - dz) % ZH) * 2 + (c ^ dc) for dc in range(2) for dz in range(ZH)]
    starts = [((x + d) % SUBS) * quarter + t * ROWS for d in range(SUBS) for t in in_order]
    q_send = rearrange(w_query, starts, 0, (quarter, ROWS), SUBS)
    q_send, o_blocks = lax.optimization_barrier((q_send, o_blocks))
    q_blocks = [None] * SUBS
    for d in range(SUBS):
        q_blocks[(-d) % SUBS] = over_x(q_send[d], every, d) if d else q_send[d]
    w_back = jnp.concatenate(o_blocks, axis=0)
    w_kv = jnp.concatenate([k_weight[0], v_weight[0]], axis=1)
    w_kv_later = jnp.concatenate(
        [lax.dynamic_slice_in_dim(w_kv, t * ROWS, ROWS, 0) for t in in_order], axis=0
    )
    gain_row = lax.dynamic_index_in_dim(norm_gain, layer_idx, 0, keepdims=False)
    gain = jnp.concatenate(
        [lax.dynamic_slice_in_dim(gain_row, x * quarter + t * ROWS, ROWS, 0) for t in in_order]
    ).astype(F32)[None, :]
    fed = None
    if PIECES > 1:
        for k in range(4):
            got = send(
                hid[span:, k * ROWS : (k + 1) * ROWS],
                [LAYERS - 1],
                lambda l, xx, zz, cc: (l, xx, 2 * cc + k // 2, k % 2) if zz == xx else None,
            )
            fed = got if fed is None else fed + got

    def first_projections():
        squares = jnp.zeros((span,), F32)
        query = jnp.zeros((span, ROWS), F32)
        block = 4 * ROWS
        for piece, t in zip(near + far, in_order):
            now = piece.astype(F32)
            squares = squares + jnp.sum(now * now, axis=1)
            gain_now = lax.dynamic_slice_in_dim(gain_row, t * block, block, 0).astype(F32)
            scaled = (now * gain_now[None, :]).astype(BF16)
            query = query + dot(scaled, lax.dynamic_slice_in_dim(w_query, t * block, block, 0))
        place = (z - x) % ZH
        own = []
        for pieces in (near, far):
            own.append(lax.select_n(place, *pieces))
        own = jnp.concatenate(
            [jnp.where(c == 0, own[0], own[1]), jnp.where(c == 0, own[1], own[0])], axis=1
        )
        gain_own = lax.dynamic_slice_in_dim(gain_row, x * quarter, quarter, 0).astype(F32)
        scaled = (own.astype(F32) * gain_own[None, :]).astype(BF16)
        kv = dot(scaled, w_kv)
        sent, _ = lax.optimization_barrier((kv.astype(BF16), o_blocks))
        for d in range(1, SUBS):
            kv = kv + over_x(sent, every, d).astype(F32)
        share = lax.dynamic_slice_in_dim(own, (z * 2 + c) * ROWS, ROWS, 1)
        return share, jnp.concatenate([query, kv], axis=1), squares

    def projections(pieces):
        own_core = jnp.concatenate(pieces, axis=1)
        other = over_core(own_core, every)
        qkv, *payloads, sums = project(own_core, other, gain, q_blocks, w_kv_later)
        squares = sums[0]
        for d in range(1, SUBS):
            got = over_x(payloads[d - 1], every, d).astype(F32)
            qkv = qkv + got[:span]
            squares = squares + got[span, :span] + got[span + 1, :span]
        return pieces[0], qkv, squares

    kv_buf = jnp.zeros((tokens, 2 * HEAD_DIM), BF16)
    pieces = None
    last_parts = []
    for step in range(LAYERS + PIECES - 1):
        micro_raw = step - layer_idx
        active = (micro_raw >= 0) & (micro_raw < PIECES)
        col_start = jnp.clip(micro_raw, 0, PIECES - 1) * span
        share, qkv, squares = projections(pieces) if step else first_projections()
        qkv = qkv * lax.rsqrt(squares / features + NORM_EPS)[:, None]

        cos_now = lax.dynamic_slice_in_dim(cos_table, col_start, span, 0)
        sin_now = lax.dynamic_slice_in_dim(sin_table, col_start, span, 0)
        mask_now = lax.dynamic_slice_in_dim(key_mask, col_start, span, 0)
        query = [
            rotate_pairs(qkv[:, i * HEAD_DIM : (i + 1) * HEAD_DIM], cos_now, sin_now).astype(BF16)
            for i in range(2)
        ]
        key_new = rotate_pairs(qkv[:, 2 * HEAD_DIM : 3 * HEAD_DIM], cos_now, sin_now).astype(BF16)
        kv_new = jnp.concatenate([key_new, qkv[:, 3 * HEAD_DIM :].astype(BF16)], axis=1)
        kv_now = lax.dynamic_update_slice_in_dim(kv_buf, kv_new, col_start, 0)
        kv_buf = jnp.where(active, kv_now, kv_buf)
        heads = []
        for i in range(2):
            scores = lax.dot_general(
                query[i],
                kv_now[:, :HEAD_DIM],
                (((1,), (1,)), ((), ())),
                preferred_element_type=F32,
            ) / math.sqrt(HEAD_DIM)
            exp_scores = jnp.where(mask_now, jnp.exp(scores), 0.0)
            probs = (exp_scores / jnp.sum(exp_scores, axis=-1, keepdims=True)).astype(BF16)
            heads.append(dot(probs, kv_now[:, HEAD_DIM:]).astype(BF16))
        attended = jnp.concatenate(heads, axis=1)

        heads = [None] * SUBS
        for d in range(SUBS):
            heads[(-d) % SUBS] = over_x(attended, every, d) if d else attended
        terms = dot(jnp.concatenate(heads, axis=1), w_back)
        half = ZH * ROWS
        summed = terms[:, :half] + over_core(terms[:, half:].astype(BF16), every).astype(F32)
        total = share.astype(F32) + summed[:, :ROWS]
        for d in range(1, ZH):
            part = summed[:, d * ROWS : (d + 1) * ROWS].astype(BF16)
            total = total + over_z(part, every, d).astype(F32)
        updated = total.astype(BF16)
        if step >= LAYERS - 1:
            last_parts.append(updated)
        if step < PIECES - 1:
            updated = jnp.where(
                layer_idx == LAYERS - 1, fed[step * span : (step + 1) * span], updated
            )
        if step < LAYERS + PIECES - 2:
            pieces = [to_next(updated, d) for d in range(ZH)]

    slots = 2 * tokens // num_reqs
    own_slots = slots // SUBS
    owner_onehot = owners[None, :] == req_ids[:, None]
    owner_starts = jnp.sum(jnp.where(owner_onehot, req_starts[None, :], 0), axis=1)
    owner_lens = jnp.sum(jnp.where(owner_onehot, lengths[None, :], 0), axis=1)
    slot_ids = x * own_slots + jnp.arange(own_slots, dtype=jnp.int32)
    row_index = jnp.where(
        slot_ids[None, :] < owner_lens[:, None], owner_starts[:, None] + slot_ids[None, :], tokens
    ).reshape(-1)
    pick = (row_index[:, None] == tok_ids[None, :]).astype(BF16)
    kv_out = dot(pick, kv_buf).astype(BF16).reshape(num_reqs, own_slots, 2 * HEAD_DIM)
    h_last = jnp.concatenate(last_parts, axis=0).reshape(num_reqs, tokens // num_reqs, ROWS)
    mixed = lax.all_to_all(jnp.concatenate([kv_out, h_last], axis=1), SECTION, 0, 0)
    kv_cache = mixed[:, :own_slots].reshape(1, LAYERS, slots, 2 * HEAD_DIM)
    h_four = mixed[(LAYERS - 1) * SUBS :, own_slots:]
    by_tp = lax.all_to_all(jnp.repeat(h_four, 2, axis=0), TP, 0, 0)
    mine = lax.dynamic_slice_in_dim(by_tp, 4 * c, 4, 0)
    final_hidden = mine.transpose(0, 2, 1).reshape(4 * ROWS, tokens // num_reqs)
    return (final_hidden, kv_cache)


def solution(mesh):
    split = Mesh(mesh.devices.reshape(2, 4, SUBS, ZH, 2), AXES)
    return jax.shard_map(
        shards,
        mesh=split,
        in_specs=(
            P(TP, None),
            P(),
            P(SECTION, None, TP),
            P(SECTION, None, TP),
            P(SECTION, None, TP),
            P(SECTION, TP, None),
            P(),
            P(),
            P(),
        ),
        out_specs=(P(TP, SECTION), P(SECTION, None, None, TP)),
        check_vma=False,
    )
```

```python
import math

import jax
import jax.numpy as jnp
from jax import lax
from jax.sharding import Mesh, PartitionSpec as P

HEAD_DIM = 128
NORM_EPS = 1e-05
ROPE_BASE = 500000.0
LAYERS = 8
SUBS = 4
ZH = 4
AXES = ("zl", "y", "x", "zh", "c")
SECTION = ("zl", "y", "x")
TP = ("zh", "c")
PIECES = 3
ROWS = 256
F32 = jnp.float32
BF16 = jnp.bfloat16


def flat(l, x, z, c):
    return ((l * SUBS + x) * ZH + z) * 2 + c


def send(value, layers, target):
    pairs = []
    for l in layers:
        for x in range(SUBS):
            for z in range(ZH):
                for c in range(2):
                    goal = target(l, x, z, c)
                    if goal is not None:
                        pairs.append((flat(l, x, z, c), flat(*goal)))
    return lax.ppermute(value, AXES, pairs)


def over_x(value, layers, d):
    return send(value, layers, lambda l, x, z, c: (l, (x + d) % SUBS, z, c))


def over_z(value, layers, d):
    return send(value, layers, lambda l, x, z, c: (l, x, (z + d) % ZH, c))


def over_core(value, layers):
    return send(value, layers, lambda l, x, z, c: (l, x, z, 1 - c))


def to_next(value, d):
    return send(
        value, range(LAYERS), lambda l, x, z, c: ((l + 1) % LAYERS, x, (z + d) % ZH, c)
    )


def rope_tables(positions):
    half_dim = HEAD_DIM // 2
    steps_i = jnp.arange(half_dim, dtype=F32)
    inv_freq = jnp.power(F32(ROPE_BASE), -(2.0 * steps_i) / HEAD_DIM)
    angle = positions.astype(F32)[:, None] * inv_freq[None, :]
    return (jnp.cos(angle), jnp.sin(angle))


def rotate_pairs(values, cos_table, sin_table):
    half_dim = values.shape[-1] // 2
    a = values[..., :half_dim]
    b = values[..., half_dim:]
    return jnp.concatenate([a * cos_table - b * sin_table, b * cos_table + a * sin_table], axis=-1)


def dot(a, b):
    return lax.dot_general(a, b, (((1,), (0,)), ((), ())), preferred_element_type=F32)


def shards(
    hidden_t, norm_gain, q_weight, k_weight, v_weight, o_weight, lengths, prior_offsets, owners
):
    zl = lax.axis_index("zl")
    x = lax.axis_index("x")
    z = lax.axis_index("zh")
    c = lax.axis_index("c")
    layer_idx = zl * 4 + lax.axis_index("y")
    tokens = hidden_t.shape[1]
    features = norm_gain.shape[1]
    quarter = features // SUBS
    span = tokens // PIECES
    num_reqs = lengths.shape[0]
    every = range(LAYERS)

    req_ends = jnp.cumsum(lengths)
    req_starts = req_ends - lengths
    tok_ids = jnp.arange(tokens, dtype=jnp.int32)
    req_ids = jnp.arange(num_reqs, dtype=jnp.int32)
    req_of_tok = jnp.sum((tok_ids[:, None] >= req_ends[None, :]).astype(jnp.int32), axis=1)
    req_onehot = req_of_tok[:, None] == req_ids[None, :]
    positions = (
        jnp.sum(jnp.where(req_onehot, (prior_offsets - req_starts)[None, :], 0), axis=1) + tok_ids
    )
    key_mask = (req_of_tok[:, None] == req_of_tok[None, :]) & (tok_ids[None, :] <= tok_ids[:, None])
    cos_table, sin_table = rope_tables(positions)

    hid = hidden_t.T
    first = hid[:span]
    near = jnp.stack([first] + [over_z(first, [0], d) for d in range(1, ZH)])
    all_first = jnp.stack([near, over_core(near, [0])])
    w_query = q_weight[0]
    w_out = o_weight[0]
    o_blocks = [None] * SUBS
    for d in range(SUBS):
        start = ((x + d) % SUBS) * quarter
        block = lax.dynamic_slice_in_dim(w_out, start, quarter, 1)
        o_blocks[(-d) % SUBS] = over_x(block, every, d) if d else block
    out_order = [((z + dz) % ZH) * 2 + (c ^ dc) for dc in range(2) for dz in range(ZH)]
    w_back = jnp.concatenate(
        [
            jnp.concatenate(
                [lax.dynamic_slice_in_dim(w, t * ROWS, ROWS, 1) for t in out_order], axis=1
            )
            for w in o_blocks
        ],
        axis=0,
    )
    w_query_later, _ = lax.optimization_barrier((w_query, o_blocks))
    q_blocks = [None] * SUBS
    for d in range(SUBS):
        start = ((x + d) % SUBS) * quarter
        block = lax.dynamic_slice_in_dim(w_query_later, start, quarter, 0)
        q_blocks[(-d) % SUBS] = over_x(block, every, d) if d else block
    in_order = [((z - dz) % ZH) * 2 + (c ^ dc) for dc in range(2) for dz in range(ZH)]
    w_in = jnp.concatenate(q_blocks + [k_weight[0], v_weight[0]], axis=1)
    w_in = jnp.concatenate(
        [lax.dynamic_slice_in_dim(w_in, t * ROWS, ROWS, 0) for t in in_order], axis=0
    )
    gain_row = lax.dynamic_index_in_dim(norm_gain, layer_idx, 0, keepdims=False)
    gain = jnp.concatenate(
        [lax.dynamic_slice_in_dim(gain_row, x * quarter + t * ROWS, ROWS, 0) for t in in_order]
    ).astype(F32)
    fed = None
    if PIECES > 1:
        for k in range(4):
            got = send(
                hid[span:, k * ROWS : (k + 1) * ROWS],
                [LAYERS - 1],
                lambda l, xx, zz, cc: (l, xx, 2 * cc + k // 2, k % 2) if zz == xx else None,
            )
            fed = got if fed is None else fed + got

    def sum_squares(h_float):
        return jnp.sum(h_float * h_float, axis=1)

    def first_projections():
        h_float = all_first.astype(F32)
        squares = jnp.zeros((span,), F32)
        query = jnp.zeros((span, ROWS), F32)
        block = 4 * ROWS
        for i, t in enumerate(in_order):
            now = h_float[i // ZH, i % ZH]
            squares = squares + sum_squares(now)
            gain_now = lax.dynamic_slice_in_dim(gain_row, t * block, block, 0).astype(F32)
            scaled = (now * gain_now[None, :]).astype(BF16)
            query = query + dot(scaled, lax.dynamic_slice_in_dim(w_query, t * block, block, 0))
        own = []
        for core in range(2):
            now = lax.dynamic_index_in_dim(all_first, c ^ core, 0, keepdims=False)
            own.append(lax.dynamic_index_in_dim(now, (z - x) % ZH, 0, keepdims=False))
        own = jnp.concatenate(own, axis=1)
        gain_own = lax.dynamic_slice_in_dim(gain_row, x * quarter, quarter, 0).astype(F32)
        scaled = (own.astype(F32) * gain_own[None, :]).astype(BF16)
        kv = dot(scaled, jnp.concatenate([k_weight[0], v_weight[0]], axis=1))
        sent = kv.astype(BF16)
        for d in range(1, SUBS):
            kv = kv + over_x(sent, every, d).astype(F32)
        share = lax.dynamic_slice_in_dim(own, (z * 2 + c) * ROWS, ROWS, 1)
        return share, jnp.concatenate([query, kv], axis=1), squares

    def projections(pieces):
        own_core = jnp.concatenate(pieces, axis=1)
        whole = jnp.concatenate([own_core, over_core(own_core, every)], axis=1)
        h_float = whole.astype(F32)
        squares = sum_squares(h_float)
        scaled = lax.optimization_barrier((h_float * gain[None, :]).astype(BF16))
        parts = dot(scaled, w_in)
        sent = parts.astype(BF16)
        high = squares.astype(BF16)
        low = (squares - high.astype(F32)).astype(BF16)
        extra = jnp.pad(jnp.stack([high, low]), ((0, 14), (0, 4 * HEAD_DIM - span)))
        qkv = jnp.concatenate([parts[:, :ROWS], parts[:, SUBS * ROWS :]], axis=1)
        for d in range(1, SUBS):
            payload = jnp.concatenate(
                [sent[:, d * ROWS : (d + 1) * ROWS], sent[:, SUBS * ROWS :]], axis=1
            )
            got = over_x(jnp.concatenate([payload, extra], axis=0), every, d).astype(F32)
            qkv = qkv + got[:span]
            squares = squares + got[span, :span] + got[span + 1, :span]
        return pieces[0], qkv, squares

    kv_buf = jnp.zeros((tokens, 2 * HEAD_DIM), BF16)
    pieces = None
    last_parts = []
    for step in range(LAYERS + PIECES - 1):
        micro_raw = step - layer_idx
        active = (micro_raw >= 0) & (micro_raw < PIECES)
        col_start = jnp.clip(micro_raw, 0, PIECES - 1) * span
        share, qkv, squares = projections(pieces) if step else first_projections()
        qkv = qkv * lax.rsqrt(squares / features + NORM_EPS)[:, None]

        cos_now = lax.dynamic_slice_in_dim(cos_table, col_start, span, 0)
        sin_now = lax.dynamic_slice_in_dim(sin_table, col_start, span, 0)
        mask_now = lax.dynamic_slice_in_dim(key_mask, col_start, span, 0)
        query = [
            rotate_pairs(qkv[:, i * HEAD_DIM : (i + 1) * HEAD_DIM], cos_now, sin_now).astype(BF16)
            for i in range(2)
        ]
        key_new = rotate_pairs(qkv[:, 2 * HEAD_DIM : 3 * HEAD_DIM], cos_now, sin_now).astype(BF16)
        kv_new = jnp.concatenate([key_new, qkv[:, 3 * HEAD_DIM :].astype(BF16)], axis=1)
        kv_now = lax.dynamic_update_slice_in_dim(kv_buf, kv_new, col_start, 0)
        kv_buf = jnp.where(active, kv_now, kv_buf)
        heads = []
        for i in range(2):
            scores = lax.dot_general(
                query[i],
                kv_now[:, :HEAD_DIM],
                (((1,), (1,)), ((), ())),
                preferred_element_type=F32,
            ) / math.sqrt(HEAD_DIM)
            exp_scores = jnp.where(mask_now, jnp.exp(scores), 0.0)
            probs = (exp_scores / jnp.sum(exp_scores, axis=-1, keepdims=True)).astype(BF16)
            heads.append(dot(probs, kv_now[:, HEAD_DIM:]).astype(BF16))
        attended = jnp.concatenate(heads, axis=1)

        heads = [None] * SUBS
        for d in range(SUBS):
            heads[(-d) % SUBS] = over_x(attended, every, d) if d else attended
        terms = dot(jnp.concatenate(heads, axis=1), w_back)
        half = ZH * ROWS
        summed = terms[:, :half] + over_core(terms[:, half:].astype(BF16), every).astype(F32)
        total = share.astype(F32) + summed[:, :ROWS]
        for d in range(1, ZH):
            part = summed[:, d * ROWS : (d + 1) * ROWS].astype(BF16)
            total = total + over_z(part, every, d).astype(F32)
        updated = total.astype(BF16)
        if step >= LAYERS - 1:
            last_parts.append(updated)
        if step < PIECES - 1:
            updated = jnp.where(
                layer_idx == LAYERS - 1, fed[step * span : (step + 1) * span], updated
            )
        if step < LAYERS + PIECES - 2:
            pieces = [to_next(updated, d) for d in range(ZH)]

    slots = 2 * tokens // num_reqs
    own_slots = slots // SUBS
    owner_onehot = owners[None, :] == req_ids[:, None]
    owner_starts = jnp.sum(jnp.where(owner_onehot, req_starts[None, :], 0), axis=1)
    owner_lens = jnp.sum(jnp.where(owner_onehot, lengths[None, :], 0), axis=1)
    slot_ids = x * own_slots + jnp.arange(own_slots, dtype=jnp.int32)
    row_index = jnp.where(
        slot_ids[None, :] < owner_lens[:, None], owner_starts[:, None] + slot_ids[None, :], tokens
    ).reshape(-1)
    pick = (row_index[:, None] == tok_ids[None, :]).astype(BF16)
    kv_out = dot(pick, kv_buf).astype(BF16).reshape(num_reqs, own_slots, 2 * HEAD_DIM)
    h_last = jnp.concatenate(last_parts, axis=0).reshape(num_reqs, tokens // num_reqs, ROWS)
    mixed = lax.all_to_all(jnp.concatenate([kv_out, h_last], axis=1), SECTION, 0, 0)
    kv_cache = mixed[:, :own_slots].reshape(1, LAYERS, slots, 2 * HEAD_DIM)
    h_four = mixed[(LAYERS - 1) * SUBS :, own_slots:]
    by_tp = lax.all_to_all(jnp.repeat(h_four, 2, axis=0), TP, 0, 0)
    mine = lax.dynamic_slice_in_dim(by_tp, 4 * c, 4, 0)
    final_hidden = mine.transpose(0, 2, 1).reshape(4 * ROWS, tokens // num_reqs)
    return (final_hidden, kv_cache)


def solution(mesh):
    split = Mesh(mesh.devices.reshape(2, 4, SUBS, ZH, 2), AXES)
    return jax.shard_map(
        shards,
        mesh=split,
        in_specs=(
            P(TP, None),
            P(),
            P(SECTION, None, TP),
            P(SECTION, None, TP),
            P(SECTION, None, TP),
            P(SECTION, TP, None),
            P(),
            P(),
            P(),
        ),
        out_specs=(P(TP, SECTION), P(SECTION, None, None, TP)),
        check_vma=False,
    )
```
